256 devices in a mesh: blk: 64 (over z, x, core), rep: 4 (over y).
Axes of the slice: x: 4, y: 4, z: 8, core: 2. Of those that a mesh axis runs over, the one named last changes fastest.
Arguments:
- samples: bfloat16 [512, 131072], P(None, 'blk'), may hold values from -6 to 6
- theta_tiles: bfloat16 [4096, 256, 256], P(('blk', 'rep')), may hold values from -6 to 6
- theta_diag: float32 [131072], P('blk'), may hold values from 0.5 to 2
- tile_row: int32 [4096], P(('blk', 'rep')), may hold values from 0 to 511, as said below
- tile_col: int32 [4096], P(('blk', 'rep')), may hold values from 0 to 7
- tile_count: int32 [256], P(('blk', 'rep')), may hold values from 4 to 16, as said below
Outputs:
- new_tiles: bfloat16 [4096, 256, 256], P(('blk', 'rep'))
- new_diag: float32 [131072], P('blk')
The draws below stay inside these ranges and needn't reach their ends.
Inputs may be any that keep to these rules, and one draw needn't show every extreme that they name: tile_row[s] differs from the slot's block column j by 1 to 8, of either sign; pairs may repeat, and repeated tiles add. Each device's live slots are its first tile_count slots; in every blk index some device is full.
All inputs are finite; a program needn't handle non-finite values.
Results may differ from the reference program's by a relative error of at most 0.0035.
Values may be sent and summed in bfloat16 or wider, within the bound.
No kernel may reach another device: no remote copies, remote signals or barrier semaphores. Data moves between devices by JAX's collectives and lax.ppermute only.
A program may use at most 128 MiB of HBM per device.

```python
import math
import jax
import jax.numpy as jnp
from jax import lax

B = 256
NS = 512
KB = 8
TCAP = 16
NB = 512
SLOTS = 4096
DEVS = 256


def pair_draw(key):
    col_key, off_key, sign_key = jax.random.split(jax.random.fold_in(key, 11), 3)
    cols = jax.random.randint(col_key, (SLOTS,), 0, KB)
    offsets = jax.random.randint(off_key, (SLOTS,), 1, KB + 1)
    signs = jax.random.randint(sign_key, (SLOTS,), 0, 2) * 2 - 1
    group = jnp.arange(SLOTS, dtype=jnp.int32) // (SLOTS // (NB // KB))
    column = group * KB + cols
    target = column + signs * offsets
    outside = jnp.logical_or(target < 0, target >= NB)
    rows = jnp.where(outside, column - signs * offsets, target)
    return (cols.astype(jnp.int32), rows.astype(jnp.int32))


def draw_tile_col(key, part):
    return pair_draw(key)[0]


def draw_tile_row(key, part):
    return pair_draw(key)[1]


def draw_tile_count(key, part):
    key = jax.random.fold_in(key, 5)
    count_key, full_key = jax.random.split(key)
    reps = DEVS // (NB // KB)
    counts = jax.random.randint(count_key, (DEVS,), TCAP // 4, TCAP + 1)
    chosen = jax.random.randint(full_key, (DEVS // reps,), 0, reps)
    full = jnp.arange(DEVS, dtype=jnp.int32) % reps == jnp.repeat(chosen, reps, total_repeat_length=DEVS)
    return jnp.where(full, TCAP, counts).astype(jnp.int32)


def levels(own_key, shape, pieces, smallest, top_value):
    level = 1.0
    for axis_at, blocks in pieces:
        steps = jax.random.uniform(jax.random.fold_in(jax.random.fold_in(own_key, 6), axis_at), (blocks,), jnp.float32, smallest / len(pieces), top_value / len(pieces))
        level = level * jnp.repeat(jnp.exp(steps), shape[axis_at] // blocks).reshape((-1,) + (1,) * (len(shape) - 1 - axis_at))
    return level


def bell_draw(own_key, extent, scale, most, cuts=(), kind=jnp.bfloat16):
    loudness = levels(own_key, extent, cuts, -0.22, 0.18) if cuts else 1.0
    entries = jax.random.normal(own_key, extent, jnp.float32) * scale * loudness
    return jnp.minimum(jnp.maximum(entries, -most), most).astype(kind)


def setup_inputs(seed: int = 0) -> dict:
    key_list = jax.random.split(jax.random.key(seed), 7)
    samples = bell_draw(key_list[0], (NS, NB * B), 1.0, 6.0, ((1, 64),))
    theta_tiles = bell_draw(key_list[1], (SLOTS, B, B), 1.0, 6.0, ((0, 256),))
    theta_diag = jnp.clip(jnp.exp(math.log(2.0) - 1.3862944 * jax.random.uniform(key_list[2], (NB * B,), jnp.float32) ** levels(key_list[2], (NB * B,), ((0, 64),), -0.2, 0.2)), 0.5, 2.0)
    tile_row = draw_tile_row(jax.random.fold_in(key_list[6], 71), 0)
    tile_col = draw_tile_col(jax.random.fold_in(key_list[6], 71), 0)
    tile_count = draw_tile_count(jax.random.fold_in(key_list[6], 71), 0)
    return dict(samples=samples, theta_tiles=theta_tiles, theta_diag=theta_diag, tile_row=tile_row, tile_col=tile_col, tile_count=tile_count)


STEP = 0.25
PENALTY = 0.5


def reference(samples, theta_tiles, theta_diag, tile_row, tile_col, tile_count):
    groups = NB // KB
    per_group = SLOTS // groups
    slot_ids = jnp.arange(SLOTS, dtype=jnp.int32)
    live = (slot_ids % TCAP) < tile_count[slot_ids // TCAP]
    tiles = jnp.where(live[:, None, None], theta_tiles, jnp.zeros_like(theta_tiles))
    padded_x = jnp.pad(samples, ((0, 0), (KB * B, KB * B)))
    columns = jnp.arange(KB, dtype=jnp.int32)

    def group_pieces(group):
        first = (group * per_group).astype(jnp.int32)
        rows = lax.dynamic_slice_in_dim(tile_row, first, per_group) - (group - 1) * KB
        cols = lax.dynamic_slice_in_dim(tile_col, first, per_group)
        part = lax.dynamic_slice_in_dim(tiles, first, per_group, 0)
        return rows.astype(jnp.int32), cols.astype(jnp.int32), part

    def group_image(group):
        rows, cols, part = group_pieces(group)
        ext = lax.dynamic_slice_in_dim(padded_x, (group * KB * B).astype(jnp.int32), 3 * KB * B, 1)
        picked = jnp.take(ext.reshape(NS, 3 * KB, B), rows, axis=1)
        prod = jnp.einsum('sta,tab->stb', picked.astype(jnp.float32), part.astype(jnp.float32))
        onehot = (cols[:, None] == columns[None, :]).astype(jnp.float32)
        summed = jnp.einsum('stb,tk->skb', prod, onehot, precision=lax.Precision.HIGHEST)
        return summed.reshape(NS, KB * B)

    parts = lax.map(group_image, jnp.arange(groups, dtype=jnp.int32))
    image_full = jnp.transpose(parts, (1, 0, 2)).reshape(NS, NB * B)
    image_full = image_full + samples.astype(jnp.float32) * theta_diag[None, :]
    image = image_full.astype(jnp.bfloat16)
    padded_w = jnp.pad(image, ((0, 0), (KB * B, KB * B)))

    def group_update(group):
        rows, cols, part = group_pieces(group)
        start = (group * KB * B).astype(jnp.int32)
        ext_x = lax.dynamic_slice_in_dim(padded_x, start, 3 * KB * B, 1).reshape(NS, 3 * KB, B)
        ext_w = lax.dynamic_slice_in_dim(padded_w, start, 3 * KB * B, 1).reshape(NS, 3 * KB, B)
        own_x = ext_x[:, KB:2 * KB]
        own_w = ext_w[:, KB:2 * KB]
        x_row = jnp.take(ext_x, rows, axis=1).astype(jnp.float32)
        w_row = jnp.take(ext_w, rows, axis=1).astype(jnp.float32)
        x_col = jnp.take(own_x, cols, axis=1).astype(jnp.float32)
        w_col = jnp.take(own_w, cols, axis=1).astype(jnp.float32)
        first = jnp.einsum('sta,stb->tab', x_row, w_col)
        second = jnp.einsum('sta,stb->tab', w_row, x_col)
        grad = (first + second) / (2.0 * NS)
        moved = part.astype(jnp.float32) - STEP * grad
        return jnp.sign(moved) * jnp.maximum(jnp.abs(moved) - STEP * PENALTY, 0.0)

    updated = lax.map(group_update, jnp.arange(groups, dtype=jnp.int32)).reshape(SLOTS, B, B)
    new_tiles = jnp.where(live[:, None, None], updated, jnp.zeros_like(updated)).astype(jnp.bfloat16)
    dots = jnp.sum(samples.astype(jnp.float32) * image.astype(jnp.float32), axis=0) / NS
    new_diag = theta_diag - STEP * (dots - 1.0 / theta_diag)
    return new_tiles, new_diag
```

```python
import functools

import jax
import jax.numpy as jnp
from jax import lax
from jax.experimental import pallas as pl
from jax.experimental.pallas import tpu as pltpu
from jax.sharding import PartitionSpec as P

B = 256
STEP = 0.25
PENALTY = 0.5
ANY = pl.BlockSpec(memory_space=pl.ANY)
VMEM = pl.BlockSpec(memory_space=pltpu.VMEM)
SMEM = pl.BlockSpec(memory_space=pltpu.SMEM)


def image_kernel(meta, src, blk, col, x_own, x_far, x_near, tiles, send_p, send_m, keep_p, keep_m, own,
                 rows_v, tiles_v, acc, row_sem, tile_sem):
    count = meta[0]
    r = meta[1]
    samples, width = acc.shape
    quarter = samples // 4
    half = quarter // 2

    def start(s, carry):
        at = pl.ds(pl.multiple_of(blk[s] * B, B), B)
        for k, ref in enumerate((x_own, x_far, x_near)):
            @pl.when(src[s] == k)
            def _():
                pltpu.make_async_copy(ref.at[:, at], rows_v.at[s], row_sem.at[s]).start()
        pltpu.make_async_copy(tiles.at[s], tiles_v.at[s], tile_sem.at[s]).start()
        return carry

    lax.fori_loop(0, count, start, 0)
    acc[...] = jnp.zeros_like(acc)

    def step(s, carry):
        pltpu.make_async_copy(x_own.at[:, pl.ds(0, B)], rows_v.at[s], row_sem.at[s]).wait()
        pltpu.make_async_copy(tiles.at[s], tiles_v.at[s], tile_sem.at[s]).wait()
        at = pl.ds(pl.multiple_of(col[s] * B, B), B)
        acc[:, at] += jnp.dot(rows_v[s], tiles_v[s], preferred_element_type=jnp.float32)
        return carry

    lax.fori_loop(0, count, step, 0)

    def part(chunk, off, rows):
        first = lax.rem(r + chunk, 4) * quarter + off
        return acc[pl.ds(pl.multiple_of(first, half), rows), :]

    send_p[:half] = part(2, half, half).astype(send_p.dtype)
    send_p[half:] = part(1, 0, half).astype(send_p.dtype)
    send_m[:half] = part(2, 0, half).astype(send_m.dtype)
    send_m[half:] = part(3, half, half).astype(send_m.dtype)
    keep_p[...] = part(1, half, half)
    keep_m[...] = part(3, 0, half)
    own[...] = part(0, 0, quarter)


def image_parts(meta, src, blk, col, x_own, x_far, x_near, tiles):
    samples, width = x_own.shape
    slots = tiles.shape[0]
    q = samples // 4
    f32, bf16 = jnp.float32, jnp.bfloat16
    return pl.pallas_call(
        image_kernel,
        out_shape=[
            jax.ShapeDtypeStruct((q, width), bf16),
            jax.ShapeDtypeStruct((q, width), bf16),
            jax.ShapeDtypeStruct((q // 2, width), f32),
            jax.ShapeDtypeStruct((q // 2, width), f32),
            jax.ShapeDtypeStruct((q, width), f32),
        ],
        in_specs=[SMEM] * 4 + [ANY] * 4,
        out_specs=[VMEM] * 5,
        scratch_shapes=[
            pltpu.VMEM((slots, samples, B), bf16),
            pltpu.VMEM((slots, B, B), bf16),
            pltpu.VMEM((samples, width), f32),
            pltpu.SemaphoreType.DMA((slots,)),
            pltpu.SemaphoreType.DMA((slots,)),
        ],
        compiler_params=pltpu.CompilerParams(vmem_limit_bytes=32 << 20),
        cost_estimate=pl.CostEstimate(flops=slots * 2 * samples * B * B, bytes_accessed=10 << 20, transcendentals=0),
        name="image_parts",
    )(meta, src, blk, col, x_own, x_far, x_near, tiles)


def grad_kernel(meta, src, blk, col, x_own, x_far, x_near, *rest):
    w_pieces = rest[:15]
    tiles, diag, out, new_diag, xv, wv, tiles_v, x_sem, w_sem, tile_sem = rest[15:]
    count = meta[0]
    r = meta[1]
    samples, width = x_own.shape
    quarter = samples // 4
    half = quarter // 2
    xs = [pltpu.make_async_copy(ref, xv.at[k], x_sem.at[k]) for k, ref in enumerate((x_own, x_far, x_near))]
    ws = []
    places = ((0, 0, quarter), (3, 0, quarter), (1, 0, quarter), (2, 0, half), (2, half, half))
    for k in range(3):
        for p, (chunk, off, rows) in enumerate(places):
            first = pl.multiple_of(lax.rem(r + chunk, 4) * quarter + off, half)
            ws.append(pltpu.make_async_copy(w_pieces[5 * k + p], wv.at[k, pl.ds(first, rows)], w_sem.at[5 * k + p]))
    tc = pltpu.make_async_copy(tiles, tiles_v, tile_sem)
    for c in xs + ws + [tc]:
        c.start()
    for c in xs + ws + [tc]:
        c.wait()

    dims = (((0,), (0,)), ((), ()))

    def step(s, carry):
        k = src[s]
        at_i = pl.ds(pl.multiple_of(blk[s] * B, B), B)
        at_j = pl.ds(pl.multiple_of(col[s] * B, B), B)
        grad = lax.dot_general(xv[k, :, at_i], wv[0, :, at_j], dims, preferred_element_type=jnp.float32)
        grad += lax.dot_general(wv[k, :, at_i], xv[0, :, at_j], dims, preferred_element_type=jnp.float32)
        moved = tiles_v[s].astype(jnp.float32) - grad * (STEP / (2.0 * samples))
        cut = STEP * PENALTY
        out[s] = (moved - jnp.clip(moved, -cut, cut)).astype(out.dtype)
        return carry

    lax.fori_loop(0, count, step, 0)

    def clear(s, carry):
        out[s] = jnp.zeros((B, B), out.dtype)
        return carry

    lax.fori_loop(count, out.shape[0], clear, 0)
    dots = jnp.sum(xv[0].astype(jnp.float32) * wv[0].astype(jnp.float32), axis=0, keepdims=True) / samples
    d = diag[...]
    new_diag[...] = d - STEP * (dots - 1.0 / d)


def updates(meta, src, blk, col, x_own, x_far, x_near, w_pieces, tiles, diag):
    samples, width = x_own.shape
    slots = tiles.shape[0]
    f32, bf16 = jnp.float32, jnp.bfloat16
    return pl.pallas_call(
        grad_kernel,
        out_shape=[
            jax.ShapeDtypeStruct(tiles.shape, bf16),
            jax.ShapeDtypeStruct((1, width), f32),
        ],
        in_specs=[SMEM] * 4 + [ANY] * 19 + [VMEM],
        out_specs=[VMEM, VMEM],
        scratch_shapes=[
            pltpu.VMEM((3, samples, width), bf16),
            pltpu.VMEM((3, samples, width), bf16),
            pltpu.VMEM(tiles.shape, bf16),
            pltpu.SemaphoreType.DMA((3,)),
            pltpu.SemaphoreType.DMA((15,)),
            pltpu.SemaphoreType.DMA,
        ],
        compiler_params=pltpu.CompilerParams(vmem_limit_bytes=40 << 20),
        cost_estimate=pl.CostEstimate(flops=slots * 4 * samples * B * B, bytes_accessed=18 << 20, transcendentals=0),
        name="updates",
    )(meta, src, blk, col, x_own, x_far, x_near, *w_pieces, tiles, diag)


def shards(samples, theta_tiles, theta_diag, tile_row, tile_col, tile_count):
    count_ns, width = samples.shape
    blocks = width // B
    groups = lax.axis_size("blk")
    reps = lax.axis_size("rep")
    group = lax.axis_index("blk")
    r = lax.axis_index("rep")
    f32, bf16 = jnp.float32, jnp.bfloat16
    half = count_ns // 8

    far = [p for g in range(1, groups - 1, 2) for p in ((g, g + 1), (g + 1, g))]
    near = [p for g in range(0, groups, 2) for p in ((g, g + 1), (g + 1, g))]
    swap_far = lambda v: lax.ppermute(v, "blk", far)
    swap_near = lambda v: lax.ppermute(v, "blk", near)
    up = lambda v: lax.ppermute(v, "rep", [(i, (i + 1) % reps) for i in range(reps)])
    down = lambda v: lax.ppermute(v, "rep", [((i + 1) % reps, i) for i in range(reps)])

    rel = tile_row // blocks - group
    even = group % 2 == 0
    src = jnp.where(rel == 0, 0, jnp.where((rel < 0) == even, 1, 2)).astype(jnp.int32)
    blk = (tile_row % blocks).astype(jnp.int32)
    col = tile_col.astype(jnp.int32)
    meta = jnp.stack([tile_count[0], r.astype(jnp.int32)])

    x_far = swap_far(samples)
    x_near = swap_near(samples)
    send_p, send_m, keep_p, keep_m, own = image_parts(meta, src, blk, col, samples, x_far, x_near, theta_tiles)
    got_p = up(send_p)
    got_m = down(send_m)
    second_p = up((keep_p + got_p[:half].astype(f32)).astype(bf16))
    second_m = down((keep_m + got_m[:half].astype(f32)).astype(bf16))
    x_mine = lax.dynamic_slice_in_dim(samples, r * (2 * half), 2 * half, 0)
    first = jnp.concatenate([got_p[half:].astype(f32) + second_m.astype(f32),
                             got_m[half:].astype(f32) + second_p.astype(f32)], axis=0)
    w_mine = (own + first + x_mine.astype(f32) * theta_diag[None, :]).astype(bf16)
    w_below = up(w_mine)
    w_above = down(w_mine)
    w_op_a = up(w_below[:half])
    w_op_b = down(w_above[half:])
    pieces = [w_mine, w_below, w_above, w_op_a, w_op_b]
    far_pieces = [swap_far(p) for p in pieces]
    near_pieces = [swap_near(p) for p in pieces]
    new_tiles, new_diag = updates(meta, src, blk, col, samples, x_far, x_near,
                                  pieces + far_pieces + near_pieces, theta_tiles, theta_diag[None, :])
    return new_tiles, new_diag.reshape(width)


def solution(mesh):
    placed = (
        P(None, "blk"),
        P(("blk", "rep"), None, None),
        P("blk"),
        P(("blk", "rep")),
        P(("blk", "rep")),
        P(("blk", "rep")),
    )
    return jax.shard_map(
        shards,
        mesh=mesh,
        in_specs=placed,
        out_specs=(P(("blk", "rep"), None, None), P("blk")),
        check_vma=False,
    )
```

```python
import functools

import jax
import jax.numpy as jnp
from jax import lax
from jax.experimental import pallas as pl
from jax.experimental.pallas import tpu as pltpu
from jax.sharding import PartitionSpec as P

B = 256
STEP = 0.25
PENALTY = 0.5
OWN, FAR, NEAR = 0, 1, 2
HBM = pl.BlockSpec(memory_space=pltpu.HBM)
VMEM = pl.BlockSpec(memory_space=pltpu.VMEM)
SMEM = pl.BlockSpec(memory_space=pltpu.SMEM)
ANY = pl.BlockSpec(memory_space=pl.ANY)
F32, BF16 = jnp.float32, jnp.bfloat16
DMA = pltpu.SemaphoreType.DMA
OVER_ROWS = (((0,), (0,)), ((), ()))
ROW_ORDER = (
    (0, 0, None), (1, 0, None), (0, 3, None), (0, 1, None), (1, 3, None), (1, 1, None),
    (0, 2, 0), (1, 2, 0), (0, 2, 1), (1, 2, 1),
)


def call(kernel, name, outs, ins, out_specs, flops, moved, scratch=(), aliases=None):
    return pl.pallas_call(
        kernel,
        out_shape=outs,
        in_specs=ins,
        out_specs=out_specs,
        scratch_shapes=scratch,
        input_output_aliases=aliases or {},
        compiler_params=pltpu.CompilerParams(vmem_limit_bytes=10 << 20),
        cost_estimate=pl.CostEstimate(flops=flops, bytes_accessed=moved, transcendentals=0),
        name=name,
    )


def like(shape, dtype):
    return jax.ShapeDtypeStruct(shape, dtype)


def block(index):
    return pl.ds(pl.multiple_of(index * B, B), B)


def each_live(count, body):
    def step(s, carry):
        body(s)
        return carry

    lax.fori_loop(0, count, step, 0)


def each_of(source, src, count, body):
    def one(s):
        @pl.when(src[s] == source)
        def _():
            body(s)

    each_live(count, one)


def over_rows(a, b):
    return lax.dot_general(a, b, OVER_ROWS, preferred_element_type=F32)


def soft(moved):
    cut = STEP * PENALTY
    return (moved - jnp.clip(moved, -cut, cut)).astype(BF16)


def load_kernel(firsts, src, *refs):
    n = len(firsts)
    copies = [
        pltpu.make_async_copy(src.at[pl.ds(first, dst.shape[0])], dst, refs[n].at[k])
        for k, (first, dst) in enumerate(zip(firsts, refs[:n], strict=True))
    ]
    for c in copies:
        c.start()
    for c in copies:
        c.wait()


def load(src, ranges):
    return call(
        functools.partial(load_kernel, [first for first, _ in ranges]), "load",
        [like((rows, src.shape[1]), src.dtype) for _, rows in ranges], [HBM], [VMEM] * len(ranges), 2 << 30, 1 << 20,
        [DMA((len(ranges),))],
    )(src)


def own_image_kernel(meta, src, blk, col, x_own, x_near, tiles, acc):
    acc[...] = jnp.zeros_like(acc)
    for source, x in ((OWN, x_own), (NEAR, x_near)):

        def add(s):
            acc[:, block(col[s])] += jnp.dot(x[:, block(blk[s])], tiles[s], preferred_element_type=F32)

        each_of(source, src, meta[0], add)


def far_image_kernel(first, meta, src, blk, col, acc, x_far, tiles, own, send_1, send_2, send_3, total):
    rows = total.shape[0]
    part = rows // 4
    total[...] = acc[first : first + rows, :]

    def add(s):
        total[:, block(col[s])] += jnp.dot(x_far[:, block(blk[s])], tiles[s], preferred_element_type=F32)

    each_of(FAR, src, meta[0], add)
    for k, out in enumerate((own, send_1, send_2, send_3)):
        at = pl.ds(pl.multiple_of(lax.rem(meta[1] + k, 4) * part, part), part)
        out[...] = total[at, :].astype(out.dtype)


def combined(first, meta, own, got, samples, diag):
    part = own.shape[0]
    at = pl.ds(pl.multiple_of(first + meta[1] * part, part), part)
    total = own[...]
    for other in got:
        total += other[:part, :].astype(F32)
    return (total + samples[at, :].astype(F32) * diag[...]).astype(BF16)


def first_combine_kernel(meta, own, got_1, got_2, got_3, samples, diag, mine):
    mine[...] = combined(0, meta, own, (got_1, got_2, got_3), samples, diag)


def second_combine_kernel(first, meta, own, got_1, got_2, got_3, samples, diag, below, above, _, __, mine, second):
    part = own.shape[0]
    mine[...] = combined(first, meta, own, (got_1, got_2, got_3), samples, diag)
    second[:part, :] = mine[...]
    second[part : 2 * part, :] = below[...]
    second[2 * part :, :] = above[...]


def stack_kernel(second, below, above, _, go_up, go_down):
    part = below.shape[0]
    half = part // 2
    go_up[:half, :] = second[part : part + half, :]
    go_up[half:, :] = below[:half, :]
    go_down[:half, :] = second[2 * part + half :, :]
    go_down[half:, :] = above[half:, :]


def join_kernel(mine, second, below, above, op_a, op_b, _, out, last):
    at = 0
    for piece in (mine, second, below, above, op_a, op_b):
        out[at : at + piece.shape[0], :] = piece[...]
        at += piece.shape[0]
    last[...] = out[at // 2 :, :]


def reorder_kernel(meta, x_own, x_far0, x_far1, x_near, out):
    rows = x_far0.shape[0]
    part = rows // 4
    to = 0
    for c, rep, half in ROW_ORDER:
        size = part if half is None else part // 2
        at = pl.multiple_of(lax.rem(meta[1] + rep, 4) * part + (half or 0) * size, size)
        out[OWN, to : to + size, :] = x_own[pl.ds(c * rows + at, size), :]
        out[FAR, to : to + size, :] = (x_far0, x_far1)[c][pl.ds(at, size), :]
        out[NEAR, to : to + size, :] = x_near[pl.ds(c * rows + at, size), :]
        to += size


def pairs(count, body):
    def step(t, carry):
        body(2 * t)
        body(2 * t + 1)
        return carry

    lax.fori_loop(0, (count + 1) // 2, step, 0)


def gradient(s, rows, src, blk, col, x, w):
    at_i, at_j = block(blk[s]), block(col[s])
    one = over_rows(x[src[s], rows, at_i], w[:, at_j])
    two = over_rows(w[:, at_i], x[OWN, rows, at_j])
    return one + jnp.where(src[s] == OWN, two, 0.0)


def column_dots(x, w):
    return jnp.sum(x.astype(F32) * w.astype(F32), axis=0, keepdims=True)


def first_update_kernel(meta, src, blk, col, x, w_mine, w_most, acc, dots, w):
    rows, cut = w.shape[0], w_mine.shape[0]
    w[:cut, :] = w_mine[...]
    w[cut:, :] = w_most[...]

    def add(s):
        acc[s] = gradient(s, slice(0, rows), src, blk, col, x, w)

    pairs(meta[0], add)
    dots[...] = column_dots(x[OWN, :rows], w[...])


def own_update_kernel(meta, src, blk, col, x, w_all, acc, tiles, diag, dots, out, moved, new_diag, out_v, sem):
    samples = x.shape[1]
    slots = tiles.shape[0]
    rows = slice(samples // 2, samples)
    w = w_all.at[samples // 2 :]
    scale = STEP / (2.0 * samples)
    save = lambda s: pltpu.make_async_copy(out_v.at[s], out.at[s], sem.at[s])

    def finish(s):
        value = tiles[s].astype(F32) - (acc[s] + gradient(s, rows, src, blk, col, x, w)) * scale
        moved[s] = value
        out_v[s] = jnp.where(s < meta[0], soft(value), jnp.zeros((B, B), BF16))

    pairs(meta[0], finish)

    def clear(s, carry):
        out_v[s] = jnp.zeros((B, B), out.dtype)
        return carry

    lax.fori_loop(meta[0], slots, clear, 0)

    def each_done(body):
        def one(s, carry):
            @pl.when(jnp.logical_or(s >= meta[0], src[s] == OWN))
            def _():
                body(s)

            return carry

        lax.fori_loop(0, slots, one, 0)

    each_done(lambda s: save(s).start())
    total = dots[...] + column_dots(x[OWN, rows], w[...])
    d = diag[...]
    new_diag[...] = d - STEP * (total / samples - 1.0 / d)
    each_done(lambda s: save(s).wait())


def other_update_kernel(source, meta, src, blk, col, x, moved, *rest):
    *pieces, _, out, w, out_v, sem = rest
    scale = STEP / (2.0 * x.shape[1])
    if len(pieces) == 1:
        w = pieces[0]
    else:
        at = 0
        for piece in pieces:
            w[at : at + piece.shape[0], :] = piece[...]
            at += piece.shape[0]
    save = lambda s: pltpu.make_async_copy(out_v.at[s], out.at[s], sem.at[s])

    def finish(s):
        grad = over_rows(w[:, block(blk[s])], x[OWN, :, block(col[s])])
        out_v[s] = soft(moved[s] - grad * scale)
        save(s).start()

    each_of(source, src, meta[0], finish)
    each_of(source, src, meta[0], lambda s: save(s).wait())


def shards(samples, theta_tiles, theta_diag, tile_row, tile_col, tile_count):
    count_ns, width = samples.shape
    blocks = width // B
    slots = theta_tiles.shape[0]
    groups = lax.axis_size("blk")
    reps = lax.axis_size("rep")
    group = lax.axis_index("blk")
    r = lax.axis_index("rep")
    rows = count_ns // 2
    part = rows // 4
    dot = 2 * count_ns * B * B

    far = [p for g in range(1, groups - 1, 2) for p in ((g, g + 1), (g + 1, g))]
    near = [p for g in range(0, groups, 2) for p in ((g, g + 1), (g + 1, g))]
    swap_far = lambda v: lax.ppermute(v, "blk", far)
    swap_near = lambda v: lax.ppermute(v, "blk", near)
    up = lambda v, n: lax.ppermute(v, "rep", [(i, (i + n) % reps) for i in range(reps)])

    rel = tile_row // blocks - group
    even = group % 2 == 0
    src = jnp.where(rel == 0, OWN, jnp.where((rel < 0) == even, FAR, NEAR)).astype(jnp.int32)
    blk = (tile_row % blocks).astype(jnp.int32)
    col = tile_col.astype(jnp.int32)
    meta = jnp.stack([tile_count[0], r.astype(jnp.int32)])
    index = (meta, src, blk, col)
    diag = theta_diag[None, :]

    x_near = swap_near(samples)
    (x_half,) = load(samples, [(0, rows)])
    x_own, x_half1 = load(samples, [(0, count_ns), (rows, rows)])
    x_far = [swap_far(x_half), swap_far(x_half1)]

    acc = call(
        own_image_kernel, "own_image", like((count_ns, width), F32), [SMEM] * 4 + [VMEM] * 3, VMEM,
        slots * dot, 4 << 20,
    )(*index, x_own, x_near, theta_tiles)

    parts = [
        call(
            functools.partial(far_image_kernel, c * rows), "far_image",
            [like((part, width), F32)] + [like((part, width), BF16)] * 3,
            [SMEM] * 4 + [VMEM] * 3, [VMEM] * 4, slots * dot // 4, 1 << 20,
            [pltpu.VMEM((rows, width), F32)],
        )(*index, acc, x_far[c], theta_tiles)
        for c in range(2)
    ]
    x_all = call(
        reorder_kernel, "reorder", like((3, count_ns, width), BF16), [SMEM] + [VMEM] * 4, VMEM, 0, 2 << 20,
    )(meta, x_own, *x_far, x_near)
    (own_0, *sends_0), (own_1, *sends_1) = parts
    got_0 = [up(send, k + 1) for k, send in enumerate(sends_0)]
    got_1 = [up(send, k + 1) for k, send in enumerate(sends_1)]
    mine_0 = call(
        first_combine_kernel, "combine", like((part, width), BF16), [SMEM] + [VMEM] * 6, VMEM, 0, 1 << 20,
    )(meta, own_0, *got_0, x_own, diag)
    far_first = swap_far(mine_0)
    mine_1, second = call(
        functools.partial(second_combine_kernel, rows), "combine",
        [like((part, width), BF16), like((3 * part, width), BF16)],
        [SMEM] + [VMEM] * 8 + [ANY] * 2, [VMEM] * 2, 0, 1 << 20,
    )(meta, own_1, *got_1, x_own, diag, up(mine_0, 1), up(mine_0, 3), far_first, x_all)
    far_second = swap_far(second)
    below, above = up(mine_1, 1), up(mine_1, 3)

    acc, dots = call(
        first_update_kernel, "first_update",
        [like(theta_tiles.shape, F32), like((1, width), F32)],
        [SMEM] * 4 + [VMEM] * 3, [VMEM] * 2, slots * dot, 4 << 20,
        [pltpu.VMEM((rows, width), BF16)],
    )(*index, x_all, mine_0, second)

    go_up, go_down = call(
        stack_kernel, "stack", [like((part, width), BF16)] * 2, [VMEM] * 3 + [ANY], [VMEM] * 2, 0, 1 << 20,
    )(second, below, above, acc)
    op_a, op_b = up(go_up, 1), up(go_down, 3)
    w_all, last = call(
        join_kernel, "join", [like((count_ns, width), BF16), like((rows, width), BF16)],
        [VMEM] * 6 + [ANY], [VMEM] * 2, 0, 1 << 20,
    )(mine_0, second, below, above, op_a, op_b, far_second)
    far_last = swap_far(last)
    w_near = swap_near(w_all)

    new_tiles, moved, new_diag = call(
        own_update_kernel, "own_update",
        [like(theta_tiles.shape, BF16), like(theta_tiles.shape, F32), like((1, width), F32)],
        [SMEM] * 4 + [VMEM] * 6, [HBM, VMEM, VMEM], slots * dot, 4 << 20,
        [pltpu.VMEM(theta_tiles.shape, BF16), DMA((slots,))],
    )(*index, x_all, w_all, acc, theta_tiles, diag, dots)

    far_pieces = [far_first, far_second, far_last]
    for source, pieces in ((NEAR, [w_near]), (FAR, far_pieces)):
        new_tiles = call(
            functools.partial(other_update_kernel, source), "other_update", like(theta_tiles.shape, BF16),
            [SMEM] * 4 + [VMEM] * (2 + len(pieces)) + [HBM], HBM, slots * dot // 4, 2 << 20,
            [pltpu.VMEM((count_ns, width), BF16), pltpu.VMEM(theta_tiles.shape, BF16), DMA((slots,))],
            {6 + len(pieces): 0},
        )(*index, x_all, moved, *pieces, new_tiles)
    return new_tiles, new_diag.reshape(width)


def solution(mesh):
    placed = (
        P(None, "blk"),
        P(("blk", "rep"), None, None),
        P("blk"),
        P(("blk", "rep")),
        P(("blk", "rep")),
        P(("blk", "rep")),
    )
    return jax.shard_map(
        shards,
        mesh=mesh,
        in_specs=placed,
        out_specs=(P(("blk", "rep"), None, None), P("blk")),
        check_vma=False,
    )
```

```python
import functools

import jax
import jax.numpy as jnp
from jax import lax
from jax.experimental import pallas as pl
from jax.experimental.pallas import tpu as pltpu
from jax.sharding import PartitionSpec as P

B = 256
STEP = 0.25
PENALTY = 0.5
OWN, FAR, NEAR = 0, 1, 2
HBM = pl.BlockSpec(memory_space=pltpu.HBM)
VMEM = pl.BlockSpec(memory_space=pltpu.VMEM)
SMEM = pl.BlockSpec(memory_space=pltpu.SMEM)
ANY = pl.BlockSpec(memory_space=pl.ANY)
F32, BF16 = jnp.float32, jnp.bfloat16
DMA = pltpu.SemaphoreType.DMA
OVER_ROWS = (((0,), (0,)), ((), ()))
REPS = (0, 3, 1, 2)
CHUNKS = (256, 256)


def call(kernel, name, outs, ins, out_specs, flops, moved, scratch=(), aliases=None, vmem=10):
    return pl.pallas_call(
        kernel,
        out_shape=outs,
        in_specs=ins,
        out_specs=out_specs,
        scratch_shapes=scratch,
        input_output_aliases=aliases or {},
        compiler_params=pltpu.CompilerParams(vmem_limit_bytes=vmem << 20),
        cost_estimate=pl.CostEstimate(flops=flops, bytes_accessed=moved, transcendentals=0),
        name=name,
    )


def like(shape, dtype):
    return jax.ShapeDtypeStruct(shape, dtype)


def block(index):
    return pl.ds(pl.multiple_of(index * B, B), B)


def each_live(count, body):
    def step(s, carry):
        body(s)
        return carry

    lax.fori_loop(0, count, step, 0)


def each_of(source, src, count, body):
    def one(s):
        @pl.when(src[s] == source)
        def _():
            body(s)

    each_live(count, one)


def over_rows(a, b):
    return lax.dot_general(a, b, OVER_ROWS, preferred_element_type=F32)


def soft(moved):
    cut = STEP * PENALTY
    return (moved - jnp.clip(moved, -cut, cut)).astype(BF16)


def load_kernel(firsts, src, *refs):
    n = len(firsts)
    copies = [
        pltpu.make_async_copy(src.at[pl.ds(first, dst.shape[0])], dst, refs[n].at[k])
        for k, (first, dst) in enumerate(zip(firsts, refs[:n], strict=True))
    ]
    for c in copies:
        c.start()
    for c in copies:
        c.wait()


def load(src, ranges, vmem):
    return call(
        functools.partial(load_kernel, [first for first, _ in ranges]), "load",
        [like((rows, src.shape[1]), src.dtype) for _, rows in ranges], [HBM], [VMEM] * len(ranges), 2 << 30, 1 << 20,
        [DMA((len(ranges),))], vmem=vmem,
    )(src)


def own_image_kernel(first, meta, src, blk, col, x_own, x_near, tiles, acc):
    rows = pl.ds(first, acc.shape[0])
    acc[...] = jnp.zeros_like(acc)
    for source, x in ((OWN, x_own), (NEAR, x_near)):

        def add(s):
            acc[:, block(col[s])] += jnp.dot(x[rows, block(blk[s])], tiles[s], preferred_element_type=F32)

        each_of(source, src, meta[0], add)


def far_image_kernel(meta, src, blk, col, acc, x_far, tiles, own, send_1, send_2, send_3, total):
    rows = total.shape[0]
    part = rows // 4
    total[...] = acc[...]

    def add(s):
        total[:, block(col[s])] += jnp.dot(x_far[:, block(blk[s])], tiles[s], preferred_element_type=F32)

    each_of(FAR, src, meta[0], add)
    for k, out in enumerate((own, send_1, send_2, send_3)):
        at = pl.ds(pl.multiple_of(lax.rem(meta[1] + k, 4) * part, part), part)
        out[...] = total[at, :].astype(out.dtype)


def combined(first, meta, own, got, samples, diag):
    part = own.shape[0]
    at = pl.ds(pl.multiple_of(first + meta[1] * part, part), part)
    total = own[...]
    for other in got:
        total += other[:part, :].astype(F32)
    return (total + samples[at, :].astype(F32) * diag[...]).astype(BF16)


def combine_kernel(first, joined, meta, own, got_1, got_2, got_3, samples, diag, *refs):
    out = refs[-1]
    if joined:
        out[:joined, :] = refs[0][...]
    out[joined:, :] = combined(first, meta, own, (got_1, got_2, got_3), samples, diag)


def stack_kernel(mine, below, above, most, rest, go_up, go_down):
    part = below.shape[0]
    half = part // 2
    for n, piece in enumerate((mine, below, above)):
        most[n * part : (n + 1) * part, :] = piece[...]
    rest[...] = most[most.shape[0] - rest.shape[0] :, :]
    go_up[...] = below[:half, :]
    go_down[...] = above[half:, :]


def join_kernel(op_a, op_b, _, out):
    half = op_a.shape[0]
    out[:half, :] = op_a[...]
    out[half:, :] = op_b[...]


def reorder_kernel(meta, x_own, x_near, *refs):
    *x_far, out = refs
    to = 0
    for rep in REPS:
        first = 0
        for far in x_far:
            rows = far.shape[0]
            part = rows // 4
            at = pl.multiple_of(lax.rem(meta[1] + rep, 4) * part, part)
            out[OWN, to : to + part, :] = x_own[pl.ds(first + at, part), :]
            out[FAR, to : to + part, :] = far[pl.ds(at, part), :]
            out[NEAR, to : to + part, :] = x_near[pl.ds(first + at, part), :]
            to += part
            first += rows


def pairs(count, body):
    def step(t, carry):
        body(2 * t)
        body(2 * t + 1)
        return carry

    lax.fori_loop(0, (count + 1) // 2, step, 0)


def gradient(s, rows, src, blk, col, x, w_own, w_near):
    k = src[s]
    at_i, at_j = block(blk[s]), block(col[s])
    one = over_rows(x[k, rows, at_i], w_own[:, at_j])
    two = over_rows(jnp.where(k == NEAR, w_near[:, at_i], w_own[:, at_i]), x[OWN, rows, at_j])
    return one + jnp.where(k == FAR, 0.0, two)


def column_dots(x, w):
    return jnp.sum(x.astype(F32) * w.astype(F32), axis=0, keepdims=True)


def first_update_kernel(meta, src, blk, col, x, w_own, w_near, acc, dots):
    rows = slice(0, w_own.shape[0])

    def add(s):
        acc[s] = gradient(s, rows, src, blk, col, x, w_own, w_near)

    pairs(meta[0], add)
    dots[...] = column_dots(x[OWN, rows], w_own[...])


def own_update_kernel(meta, src, blk, col, x, w_op, near_op, acc, tiles, diag, dots, out, moved, new_diag, out_v, sem):
    samples = x.shape[1]
    slots = tiles.shape[0]
    rows = slice(samples - w_op.shape[0], samples)
    scale = STEP / (2.0 * samples)
    count = meta[0]
    even = (count + 1) // 2 * 2
    save = lambda s: pltpu.make_async_copy(out_v.at[s], out.at[s], sem.at[s])

    def clear(s, carry):
        out_v[s] = jnp.zeros((B, B), out.dtype)
        save(s).start()
        return carry

    lax.fori_loop(even, slots, clear, 0)

    def done_here(s):
        return jnp.logical_or(s >= count, src[s] != FAR)

    def finish(s):
        value = tiles[s].astype(F32) - (acc[s] + gradient(s, rows, src, blk, col, x, w_op, near_op)) * scale
        moved[s] = value
        out_v[s] = jnp.where(s < count, soft(value), jnp.zeros((B, B), BF16))

    def step(t, carry):
        finish(2 * t)
        finish(2 * t + 1)
        for s in (2 * t, 2 * t + 1):

            @pl.when(done_here(s))
            def _():
                save(s).start()

        return carry

    lax.fori_loop(0, even // 2, step, 0)
    total = dots[...] + column_dots(x[OWN, rows], w_op[...])
    d = diag[...]
    new_diag[...] = d - STEP * (total / samples - 1.0 / d)

    def end(s, carry):
        @pl.when(done_here(s))
        def _():
            save(s).wait()

        return carry

    lax.fori_loop(0, slots, end, 0)


def far_update_kernel(meta, src, blk, col, x, moved, *rest):
    *pieces, _, out, w, out_v, sem = rest
    scale = STEP / (2.0 * x.shape[1])
    at = 0
    for piece in pieces:
        w[at : at + piece.shape[0], :] = piece[...]
        at += piece.shape[0]
    save = lambda s: pltpu.make_async_copy(out_v.at[s], out.at[s], sem.at[s])

    def finish(s):
        grad = over_rows(w[:, block(blk[s])], x[OWN, :, block(col[s])])
        out_v[s] = soft(moved[s] - grad * scale)
        save(s).start()

    each_of(FAR, src, meta[0], finish)
    each_of(FAR, src, meta[0], lambda s: save(s).wait())


def shards(samples, theta_tiles, theta_diag, tile_row, tile_col, tile_count):
    count_ns, width = samples.shape
    blocks = width // B
    slots = theta_tiles.shape[0]
    groups = lax.axis_size("blk")
    reps = lax.axis_size("rep")
    group = lax.axis_index("blk")
    r = lax.axis_index("rep")
    quarter = count_ns // 4
    firsts = [sum(CHUNKS[:c]) for c in range(len(CHUNKS))]
    dot = 2 * count_ns * B * B

    far = [p for g in range(1, groups - 1, 2) for p in ((g, g + 1), (g + 1, g))]
    near = [p for g in range(0, groups, 2) for p in ((g, g + 1), (g + 1, g))]
    swap_far = lambda v: lax.ppermute(v, "blk", far)
    swap_near = lambda v: lax.ppermute(v, "blk", near)
    up = lambda v, n: lax.ppermute(v, "rep", [(i, (i + n) % reps) for i in range(reps)])

    rel = tile_row // blocks - group
    even = group % 2 == 0
    src = jnp.where(rel == 0, OWN, jnp.where((rel < 0) == even, FAR, NEAR)).astype(jnp.int32)
    blk = (tile_row % blocks).astype(jnp.int32)
    col = tile_col.astype(jnp.int32)
    meta = jnp.stack([tile_count[0], r.astype(jnp.int32)])
    index = (meta, src, blk, col)
    diag = theta_diag[None, :]

    x_near = swap_near(samples)
    (x_first,) = load(samples, [(0, CHUNKS[0])], 62)
    x_own, *x_rest = load(samples, [(0, count_ns), *zip(firsts[1:], CHUNKS[1:], strict=True)], 10)
    x_far = [swap_far(x) for x in (x_first, *x_rest)]

    accs = [
        call(
            functools.partial(own_image_kernel, first), "own_image", like((rows, width), F32),
            [SMEM] * 4 + [VMEM] * 3, VMEM, slots * dot, 4 << 20,
        )(*index, x_own, x_near, theta_tiles)
        for first, rows in zip(firsts, CHUNKS, strict=True)
    ]
    x_all = call(
        reorder_kernel, "reorder", like((3, count_ns, width), BF16), [SMEM] + [VMEM] * (2 + len(CHUNKS)), VMEM,
        0, 2 << 20,
    )(meta, x_own, x_near, *x_far)

    joined, done, before = [], 0, []
    for c, (first, rows) in enumerate(zip(firsts, CHUNKS, strict=True)):
        part = rows // 4
        own, *sends = call(
            far_image_kernel, "far_image",
            [like((part, width), F32)] + [like((part, width), BF16)] * 3,
            [SMEM] * 4 + [VMEM] * 3, [VMEM] * 4, slots * dot // 4, 1 << 20,
            [pltpu.VMEM((rows, width), F32)],
        )(*index, accs[c], x_far[c], theta_tiles)
        got = [up(send, k + 1) for k, send in enumerate(sends)]
        if c + 1 == len(CHUNKS):
            far_first = swap_far(joined[0])
            before = [far_first, x_all]
        joined = [
            call(
                functools.partial(combine_kernel, first, done), "combine", like((done + part, width), BF16),
                [SMEM] + [VMEM] * (6 + len(joined)) + [ANY] * len(before), VMEM, 0, 1 << 20,
            )(meta, own, *got, x_own, diag, *joined, *before)
        ]
        done += part
    w_mine = joined[0]
    w_most, w_rest, go_up, go_down = call(
        stack_kernel, "stack",
        [like((3 * quarter, width), BF16), like((2 * quarter + part, width), BF16)]
        + [like((quarter // 2, width), BF16)] * 2,
        [VMEM] * 3, [VMEM] * 4, 0, 1 << 20,
    )(w_mine, up(w_mine, 1), up(w_mine, 3))
    far_rest, near_most = swap_far(w_rest), swap_near(w_most)
    op_a, op_b = up(go_up, 1), up(go_down, 3)

    acc, dots = call(
        first_update_kernel, "first_update",
        [like(theta_tiles.shape, F32), like((1, width), F32)],
        [SMEM] * 4 + [VMEM] * 3, [VMEM] * 2, slots * dot, 4 << 20,
    )(*index, x_all, w_most, near_most)

    w_op = call(
        join_kernel, "join", like((quarter, width), BF16), [VMEM] * 2 + [ANY], VMEM, 0, 1 << 20,
    )(op_a, op_b, acc)
    far_op = swap_far(w_op)

    new_tiles, moved, new_diag = call(
        own_update_kernel, "own_update",
        [like(theta_tiles.shape, BF16), like(theta_tiles.shape, F32), like((1, width), F32)],
        [SMEM] * 4 + [VMEM] * 7, [HBM, VMEM, VMEM], slots * dot, 4 << 20,
        [pltpu.VMEM(theta_tiles.shape, BF16), DMA((slots,))],
    )(*index, x_all, w_op, swap_near(w_op), acc, theta_tiles, diag, dots)

    far_pieces = [far_first, far_rest, far_op]
    new_tiles = call(
        far_update_kernel, "far_update", like(theta_tiles.shape, BF16),
        [SMEM] * 4 + [VMEM] * (2 + len(far_pieces)) + [HBM], HBM, slots * dot // 4, 2 << 20,
        [pltpu.VMEM((count_ns, width), BF16), pltpu.VMEM(theta_tiles.shape, BF16), DMA((slots,))],
        {6 + len(far_pieces): 0},
    )(*index, x_all, moved, *far_pieces, new_tiles)
    return new_tiles, new_diag.reshape(width)


def solution(mesh):
    placed = (
        P(None, "blk"),
        P(("blk", "rep"), None, None),
        P("blk"),
        P(("blk", "rep")),
        P(("blk", "rep")),
        P(("blk", "rep")),
    )
    return jax.shard_map(
        shards,
        mesh=mesh,
        in_specs=placed,
        out_specs=(P(("blk", "rep"), None, None), P("blk")),
        check_vma=False,
    )
```

```python
import functools

import jax
import jax.numpy as jnp
from jax import lax
from jax.experimental import pallas as pl
from jax.experimental.pallas import tpu as pltpu
from jax.sharding import PartitionSpec as P

B = 256
STEP = 0.25
PENALTY = 0.5
OWN, FAR, NEAR = 0, 1, 2
HBM = pl.BlockSpec(memory_space=pltpu.HBM)
VMEM = pl.BlockSpec(memory_space=pltpu.VMEM)
SMEM = pl.BlockSpec(memory_space=pltpu.SMEM)
ANY = pl.BlockSpec(memory_space=pl.ANY)
F32, BF16 = jnp.float32, jnp.bfloat16
DMA = pltpu.SemaphoreType.DMA
OVER_ROWS = (((0,), (0,)), ((), ()))
REPS = (0, 3, 1, 2)
CHUNKS = (256, 256)


def call(kernel, name, outs, ins, out_specs, flops, moved, scratch=(), aliases=None, vmem=10):
    return pl.pallas_call(
        kernel,
        out_shape=outs,
        in_specs=ins,
        out_specs=out_specs,
        scratch_shapes=scratch,
        input_output_aliases=aliases or {},
        compiler_params=pltpu.CompilerParams(vmem_limit_bytes=int(vmem * 2**20)),
        cost_estimate=pl.CostEstimate(flops=flops, bytes_accessed=moved, transcendentals=0),
        name=name,
    )


def like(shape, dtype):
    return jax.ShapeDtypeStruct(shape, dtype)


def block(index):
    return pl.ds(pl.multiple_of(index * B, B), B)


def each_live(count, body):
    def step(s, carry):
        body(s)
        return carry

    lax.fori_loop(0, count, step, 0)


def each_of(source, src, count, body):
    def one(s):
        @pl.when(src[s] == source)
        def _():
            body(s)

    each_live(count, one)


def over_rows(a, b):
    return lax.dot_general(a, b, OVER_ROWS, preferred_element_type=F32)


def soft(moved):
    cut = STEP * PENALTY
    return (moved - jnp.clip(moved, -cut, cut)).astype(BF16)


def load_kernel(firsts, src, *refs):
    n = len(firsts)
    copies = [
        pltpu.make_async_copy(src.at[pl.ds(first, dst.shape[0])], dst, refs[n].at[k])
        for k, (first, dst) in enumerate(zip(firsts, refs[:n], strict=True))
    ]
    for c in copies:
        c.start()
    for c in copies:
        c.wait()


def load_first_kernel(src, dst, through, in_sem, out_sem):
    pieces, rows, _ = through.shape
    ins = [pltpu.make_async_copy(src.at[pl.ds(n * rows, rows)], through.at[n], in_sem.at[n]) for n in range(pieces)]
    outs = [pltpu.make_async_copy(through.at[n], dst.at[pl.ds(n * rows, rows)], out_sem.at[n]) for n in range(pieces)]
    for c in ins:
        c.start()
    for came, goes in zip(ins, outs, strict=True):
        came.wait()
        goes.start()
    for c in outs:
        c.wait()


def load_first(src, rows):
    pieces = 4
    return call(
        load_first_kernel, "load", like((rows, src.shape[1]), src.dtype), [HBM], HBM, 0, 1 << 20,
        [pltpu.VMEM((pieces, rows // pieces, src.shape[1]), src.dtype), DMA((pieces,)), DMA((pieces,))], vmem=62.5,
    )(src)


def load(src, ranges, vmem):
    return call(
        functools.partial(load_kernel, [first for first, _ in ranges]), "load",
        [like((rows, src.shape[1]), src.dtype) for _, rows in ranges], [HBM], [VMEM] * len(ranges), 2 << 30, 1 << 20,
        [DMA((len(ranges),))], vmem=vmem,
    )(src)


def far_image_kernel(meta, src, blk, col, acc, x_far, tiles, own, send_1, send_2, send_3, total):
    rows = total.shape[0]
    part = rows // 4
    total[...] = acc[...]

    def add(s):
        total[:, block(col[s])] += jnp.dot(x_far[:, block(blk[s])], tiles[s], preferred_element_type=F32)

    each_of(FAR, src, meta[0], add)
    for k, out in enumerate((own, send_1, send_2, send_3)):
        at = pl.ds(pl.multiple_of(lax.rem(meta[1] + k, 4) * part, part), part)
        out[...] = total[at, :].astype(out.dtype)


def combined(first, meta, own, got, samples, diag):
    part = own.shape[0]
    at = pl.ds(pl.multiple_of(first + meta[1] * part, part), part)
    total = own[...]
    for other in got:
        total += other[:part, :].astype(F32)
    return (total + samples[at, :].astype(F32) * diag[...]).astype(BF16)


def combine_kernel(first, joined, meta, own, got_1, got_2, got_3, samples, diag, *refs):
    out = refs[-1]
    if joined:
        out[:joined, :] = refs[0][...]
    out[joined:, :] = combined(first, meta, own, (got_1, got_2, got_3), samples, diag)


def stack_kernel(mine, below, above, most, rest, go_up, go_down):
    part = below.shape[0]
    half = part // 2
    for n, piece in enumerate((mine, below, above)):
        most[n * part : (n + 1) * part, :] = piece[...]
    rest[...] = most[most.shape[0] - rest.shape[0] :, :]
    go_up[...] = below[:half, :]
    go_down[...] = above[half:, :]


def join_kernel(op_a, op_b, _, out):
    half = op_a.shape[0]
    out[:half, :] = op_a[...]
    out[half:, :] = op_b[...]


def reorder_kernel(meta, x_own, x_near, *refs):
    *x_far, out = refs
    to = 0
    for rep in REPS:
        first = 0
        for far in x_far:
            rows = far.shape[0]
            part = rows // 4
            at = pl.multiple_of(lax.rem(meta[1] + rep, 4) * part, part)
            out[OWN, to : to + part, :] = x_own[pl.ds(first + at, part), :]
            out[FAR, to : to + part, :] = far[pl.ds(at, part), :]
            out[NEAR, to : to + part, :] = x_near[pl.ds(first + at, part), :]
            to += part
            first += rows


UNROLL = 4


def whole_steps(count):
    return (count + UNROLL - 1) // UNROLL


def in_steps(count, body):
    def step(t, carry):
        body([UNROLL * t + n for n in range(UNROLL)])
        return carry

    lax.fori_loop(0, whole_steps(count), step, 0)


def gradient(s, rows, src, blk, col, x, w_own, w_near):
    k = src[s]
    at_i, at_j = block(blk[s]), block(col[s])
    one = over_rows(x[k, rows, at_i], w_own[:, at_j])
    two = over_rows(jnp.where(k == NEAR, w_near[:, at_i], w_own[:, at_i]), x[OWN, rows, at_j])
    return one + jnp.where(k == FAR, 0.0, two)


def column_dots(x, w):
    return jnp.sum(x.astype(F32) * w.astype(F32), axis=0, keepdims=True)


def first_update_kernel(meta, src, blk, col, x, w_own, w_near, acc, dots):
    rows = slice(0, w_own.shape[0])

    def add(slots):
        for s in slots:
            acc[s] = gradient(s, rows, src, blk, col, x, w_own, w_near)

    in_steps(meta[0], add)
    dots[...] = column_dots(x[OWN, rows], w_own[...])


def own_update_kernel(meta, src, blk, col, x, w_op, near_op, acc, tiles, diag, dots, out, moved, new_diag, out_v, sem):
    samples = x.shape[1]
    slots = tiles.shape[0]
    rows = slice(samples - w_op.shape[0], samples)
    scale = STEP / (2.0 * samples)
    count = meta[0]
    whole = whole_steps(count) * UNROLL
    save = lambda s: pltpu.make_async_copy(out_v.at[s], out.at[s], sem.at[s])

    def clear(s, carry):
        out_v[s] = jnp.zeros((B, B), out.dtype)
        save(s).start()
        return carry

    lax.fori_loop(whole, slots, clear, 0)

    def done_here(s):
        return jnp.logical_or(s >= count, src[s] != FAR)

    def finish(s):
        value = tiles[s].astype(F32) - (acc[s] + gradient(s, rows, src, blk, col, x, w_op, near_op)) * scale
        moved[s] = value
        out_v[s] = jnp.where(s < count, soft(value), jnp.zeros((B, B), BF16))

    def step(some):
        for s in some:
            finish(s)
        for s in some:

            @pl.when(done_here(s))
            def _():
                save(s).start()

    in_steps(count, step)
    total = dots[...] + column_dots(x[OWN, rows], w_op[...])
    d = diag[...]
    new_diag[...] = d - STEP * (total / samples - 1.0 / d)

    def end(s, carry):
        @pl.when(done_here(s))
        def _():
            save(s).wait()

        return carry

    lax.fori_loop(0, slots, end, 0)


def own_image_kernel(first, meta, src, blk, col, x_own, x_near, tiles, acc):
    rows = pl.ds(first, acc.shape[0])
    acc[...] = jnp.zeros_like(acc)

    def add(slots):
        products = []
        for s in slots:
            at = block(blk[s])
            x = jnp.where(src[s] == NEAR, x_near[rows, at], x_own[rows, at])
            used = jnp.logical_and(s < meta[0], src[s] != FAR)
            products.append(jnp.where(used, jnp.dot(x, tiles[s], preferred_element_type=F32), 0.0))
        for s, product in zip(slots, products, strict=True):
            acc[:, block(col[s])] += product

    in_steps(meta[0], add)


def far_update_kernel(meta, src, blk, col, x, moved, *rest):
    *pieces, _, out, w, out_v, sem = rest
    scale = STEP / (2.0 * x.shape[1])
    at = 0
    for piece in pieces:
        w[at : at + piece.shape[0], :] = piece[...]
        at += piece.shape[0]
    save = lambda s: pltpu.make_async_copy(out_v.at[s], out.at[s], sem.at[s])

    def finish(s):
        grad = over_rows(w[:, block(blk[s])], x[OWN, :, block(col[s])])
        out_v[s] = soft(moved[s] - grad * scale)
        save(s).start()

    each_of(FAR, src, meta[0], finish)
    each_of(FAR, src, meta[0], lambda s: save(s).wait())


def shards(samples, theta_tiles, theta_diag, tile_row, tile_col, tile_count):
    count_ns, width = samples.shape
    blocks = width // B
    slots = theta_tiles.shape[0]
    groups = lax.axis_size("blk")
    reps = lax.axis_size("rep")
    group = lax.axis_index("blk")
    r = lax.axis_index("rep")
    quarter = count_ns // 4
    firsts = [sum(CHUNKS[:c]) for c in range(len(CHUNKS))]
    dot = 2 * count_ns * B * B

    far = [p for g in range(1, groups - 1, 2) for p in ((g, g + 1), (g + 1, g))]
    near = [p for g in range(0, groups, 2) for p in ((g, g + 1), (g + 1, g))]
    swap_far = lambda v: lax.ppermute(v, "blk", far)
    swap_near = lambda v: lax.ppermute(v, "blk", near)
    up = lambda v, n: lax.ppermute(v, "rep", [(i, (i + n) % reps) for i in range(reps)])

    rel = tile_row // blocks - group
    even = group % 2 == 0
    src = jnp.where(rel == 0, OWN, jnp.where((rel < 0) == even, FAR, NEAR)).astype(jnp.int32)
    blk = (tile_row % blocks).astype(jnp.int32)
    col = tile_col.astype(jnp.int32)
    meta = jnp.stack([tile_count[0], r.astype(jnp.int32)])
    index = (meta, src, blk, col)
    diag = theta_diag[None, :]

    x_near = swap_near(samples)
    x_first = load_first(samples, CHUNKS[0])
    x_own, *x_rest = load(samples, [(0, count_ns), *zip(firsts[1:], CHUNKS[1:], strict=True)], 10)
    x_far = [swap_far(x) for x in (x_first, *x_rest)]

    accs = [
        call(
            functools.partial(own_image_kernel, first), "own_image", like((rows, width), F32),
            [SMEM] * 4 + [VMEM] * 3, VMEM, slots * dot, 4 << 20,
        )(*index, x_own, x_near, theta_tiles)
        for first, rows in zip(firsts, CHUNKS, strict=True)
    ]
    x_all = call(
        reorder_kernel, "reorder", like((3, count_ns, width), BF16), [SMEM] + [VMEM] * (2 + len(CHUNKS)), VMEM,
        0, 2 << 20,
    )(meta, x_own, x_near, *x_far)

    joined, done, before = [], 0, []
    for c, (first, rows) in enumerate(zip(firsts, CHUNKS, strict=True)):
        part = rows // 4
        own, *sends = call(
            far_image_kernel, "far_image",
            [like((part, width), F32)] + [like((part, width), BF16)] * 3,
            [SMEM] * 4 + [VMEM] * 3, [VMEM] * 4, slots * dot // 4, 1 << 20,
            [pltpu.VMEM((rows, width), F32)],
        )(*index, accs[c], x_far[c], theta_tiles)
        got = [up(send, k + 1) for k, send in enumerate(sends)]
        if c + 1 == len(CHUNKS):
            far_first = swap_far(joined[0])
            before = [far_first, x_all]
        joined = [
            call(
                functools.partial(combine_kernel, first, done), "combine", like((done + part, width), BF16),
                [SMEM] + [VMEM] * (6 + len(joined)) + [ANY] * len(before), VMEM, 0, 1 << 20,
            )(meta, own, *got, x_own, diag, *joined, *before)
        ]
        done += part
    w_mine = joined[0]
    w_most, w_rest, go_up, go_down = call(
        stack_kernel, "stack",
        [like((3 * quarter, width), BF16), like((2 * quarter + part, width), BF16)]
        + [like((quarter // 2, width), BF16)] * 2,
        [VMEM] * 3, [VMEM] * 4, 0, 1 << 20,
    )(w_mine, up(w_mine, 1), up(w_mine, 3))
    far_rest, near_most = swap_far(w_rest), swap_near(w_most)
    op_a, op_b = up(go_up, 1), up(go_down, 3)

    acc, dots = call(
        first_update_kernel, "first_update",
        [like(theta_tiles.shape, F32), like((1, width), F32)],
        [SMEM] * 4 + [VMEM] * 3, [VMEM] * 2, slots * dot, 4 << 20,
    )(*index, x_all, w_most, near_most)

    w_op = call(
        join_kernel, "join", like((quarter, width), BF16), [VMEM] * 2 + [ANY], VMEM, 0, 1 << 20,
    )(op_a, op_b, acc)
    far_op = swap_far(w_op)

    new_tiles, moved, new_diag = call(
        own_update_kernel, "own_update",
        [like(theta_tiles.shape, BF16), like(theta_tiles.shape, F32), like((1, width), F32)],
        [SMEM] * 4 + [VMEM] * 7, [HBM, VMEM, VMEM], slots * dot, 4 << 20,
        [pltpu.VMEM(theta_tiles.shape, BF16), DMA((slots,))],
    )(*index, x_all, w_op, swap_near(w_op), acc, theta_tiles, diag, dots)

    far_pieces = [far_first, far_rest, far_op]
    new_tiles = call(
        far_update_kernel, "far_update", like(theta_tiles.shape, BF16),
        [SMEM] * 4 + [VMEM] * (2 + len(far_pieces)) + [HBM], HBM, slots * dot // 4, 2 << 20,
        [pltpu.VMEM((count_ns, width), BF16), pltpu.VMEM(theta_tiles.shape, BF16), DMA((slots,))],
        {6 + len(far_pieces): 0},
    )(*index, x_all, moved, *far_pieces, new_tiles)
    return new_tiles, new_diag.reshape(width)


def solution(mesh):
    placed = (
        P(None, "blk"),
        P(("blk", "rep"), None, None),
        P("blk"),
        P(("blk", "rep")),
        P(("blk", "rep")),
        P(("blk", "rep")),
    )
    return jax.shard_map(
        shards,
        mesh=mesh,
        in_specs=placed,
        out_specs=(P(("blk", "rep"), None, None), P("blk")),
        check_vma=False,
    )
```

```python
import functools

import jax
import jax.numpy as jnp
from jax import lax
from jax.experimental import pallas as pl
from jax.experimental.pallas import tpu as pltpu
from jax.sharding import PartitionSpec as P

B = 256
STEP = 0.25
PENALTY = 0.5
OWN, FAR, NEAR = 0, 1, 2
HBM = pl.BlockSpec(memory_space=pltpu.HBM)
VMEM = pl.BlockSpec(memory_space=pltpu.VMEM)
SMEM = pl.BlockSpec(memory_space=pltpu.SMEM)
ANY = pl.BlockSpec(memory_space=pl.ANY)
F32, BF16 = jnp.float32, jnp.bfloat16
DMA = pltpu.SemaphoreType.DMA
OVER_ROWS = (((0,), (0,)), ((), ()))
REPS = (0, 3, 1, 2)
CHUNKS = (256, 256)


def call(kernel, name, outs, ins, out_specs, flops, moved, scratch=(), aliases=None, vmem=10):
    return pl.pallas_call(
        kernel,
        out_shape=outs,
        in_specs=ins,
        out_specs=out_specs,
        scratch_shapes=scratch,
        input_output_aliases=aliases or {},
        compiler_params=pltpu.CompilerParams(vmem_limit_bytes=int(vmem * 2**20)),
        cost_estimate=pl.CostEstimate(flops=flops, bytes_accessed=moved, transcendentals=0),
        name=name,
    )


def like(shape, dtype):
    return jax.ShapeDtypeStruct(shape, dtype)


def block(index):
    return pl.ds(pl.multiple_of(index * B, B), B)


def each_live(count, body):
    def step(s, carry):
        body(s)
        return carry

    lax.fori_loop(0, count, step, 0)


def list_of(source, src, count, found):
    def clear(n, carry):
        found[n] = 0
        return carry

    def one(s, n):
        here = src[s] == source

        @pl.when(here)
        def _():
            found[n] = s

        return n + here.astype(jnp.int32)

    lax.fori_loop(0, found.shape[0], clear, 0)
    return lax.fori_loop(0, count, one, 0)


UNROLL = 4


def whole_steps(count):
    return (count + UNROLL - 1) // UNROLL


def in_steps(count, body):
    def step(t, carry):
        body([UNROLL * t + n for n in range(UNROLL)])
        return carry

    lax.fori_loop(0, whole_steps(count), step, 0)


def over_rows(a, b):
    return lax.dot_general(a, b, OVER_ROWS, preferred_element_type=F32)


def soft(moved):
    cut = STEP * PENALTY
    return (moved - jnp.clip(moved, -cut, cut)).astype(BF16)


def load_kernel(firsts, src, *refs):
    n = len(firsts)
    copies = [
        pltpu.make_async_copy(src.at[pl.ds(first, dst.shape[0])], dst, refs[n].at[k])
        for k, (first, dst) in enumerate(zip(firsts, refs[:n], strict=True))
    ]
    for c in copies:
        c.start()
    for c in copies:
        c.wait()


def load_first_kernel(src, dst, through, in_sem, out_sem):
    pieces, rows, _ = through.shape
    ins = [pltpu.make_async_copy(src.at[pl.ds(n * rows, rows)], through.at[n], in_sem.at[n]) for n in range(pieces)]
    outs = [pltpu.make_async_copy(through.at[n], dst.at[pl.ds(n * rows, rows)], out_sem.at[n]) for n in range(pieces)]
    for c in ins:
        c.start()
    for came, goes in zip(ins, outs, strict=True):
        came.wait()
        goes.start()
    for c in outs:
        c.wait()


def load_first(src, rows):
    pieces = 4
    return call(
        load_first_kernel, "load", like((rows, src.shape[1]), src.dtype), [HBM], HBM, 0, 1 << 20,
        [pltpu.VMEM((pieces, rows // pieces, src.shape[1]), src.dtype), DMA((pieces,)), DMA((pieces,))], vmem=62.5,
    )(src)


def load(src, ranges, vmem):
    return call(
        functools.partial(load_kernel, [first for first, _ in ranges]), "load",
        [like((rows, src.shape[1]), src.dtype) for _, rows in ranges], [HBM], [VMEM] * len(ranges), 2 << 30, 1 << 20,
        [DMA((len(ranges),))], vmem=vmem,
    )(src)


def far_image_kernel(meta, src, blk, col, acc, x_far, tiles, own, send_1, send_2, send_3, total, found):
    rows = total.shape[0]
    part = rows // 4
    total[...] = acc[...]

    count = list_of(FAR, src, meta[0], found)

    def add(places):
        slots = [found[n] for n in places]
        products = [jnp.dot(x_far[:, block(blk[s])], tiles[s], preferred_element_type=F32) for s in slots]
        for n, s, product in zip(places, slots, products, strict=True):
            total[:, block(col[s])] += jnp.where(n < count, product, 0.0)

    in_steps(count, add)
    for k, out in enumerate((own, send_1, send_2, send_3)):
        at = pl.ds(pl.multiple_of(lax.rem(meta[1] + k, 4) * part, part), part)
        out[...] = total[at, :].astype(out.dtype)


def combined(first, meta, own, got, samples, diag):
    part = own.shape[0]
    at = pl.ds(pl.multiple_of(first + meta[1] * part, part), part)
    total = own[...]
    for other in got:
        total += other[:part, :].astype(F32)
    return (total + samples[at, :].astype(F32) * diag[...]).astype(BF16)


def combine_kernel(first, joined, meta, own, got_1, got_2, got_3, samples, diag, *refs):
    out = refs[-1]
    if joined:
        out[:joined, :] = refs[0][...]
    out[joined:, :] = combined(first, meta, own, (got_1, got_2, got_3), samples, diag)


def stack_kernel(mine, below, above, sides, rest, go_up, go_down):
    part = below.shape[0]
    half = part // 2
    ours = rest.shape[0] - 2 * part
    rest[:ours, :] = mine[part - ours :, :]
    for out, at in ((sides, 0), (rest, ours)):
        out[at : at + part, :] = below[...]
        out[at + part : at + 2 * part, :] = above[...]
    go_up[...] = below[:half, :]
    go_down[...] = above[half:, :]


def join_kernel(op_a, op_b, out):
    half = op_a.shape[0]
    out[:half, :] = op_a[...]
    out[half:, :] = op_b[...]


def reorder_kernel(meta, x_own, x_near, *refs):
    *x_far, out, turned = refs
    spans, first = [], 0
    for far in x_far:
        spans.append((first, far.shape[0] // 4))
        first += far.shape[0]

    def places():
        for rep in REPS:
            for c, (first, part) in enumerate(spans):
                yield c, first, pl.multiple_of(lax.rem(meta[1] + rep, 4) * part, part), part

    def turn(n, carry):
        at = block(n)
        own, far, near = [], [], []
        for c, first, row, part in places():
            own.append(x_own[pl.ds(first + row, part), at])
            far.append(x_far[c][pl.ds(row, part), at])
            near.append(x_near[pl.ds(first + row, part), at])
        own = jnp.concatenate(own, axis=0)
        out[:, at] = own
        turned[OWN, at, :] = own.T
        turned[FAR, at, :] = jnp.concatenate(far, axis=0).T
        turned[NEAR, at, :] = jnp.concatenate(near, axis=0).T
        return carry

    lax.fori_loop(0, out.shape[1] // B, turn, 0)


def gradient(s, src, blk, col, x, turned, w_own, w_near):
    k = src[s]
    at_i, at_j = block(blk[s]), block(col[s])
    one = jnp.dot(turned[k, at_i, :], w_own[:, at_j], preferred_element_type=F32)
    two = over_rows(jnp.where(k == NEAR, w_near[:, at_i], w_own[:, at_i]), x[:, at_j])
    return one + jnp.where(k == FAR, 0.0, two)


def column_dots(x, w):
    return jnp.sum(x.astype(F32) * w.astype(F32), axis=0, keepdims=True)


def own_update_kernel(meta, src, blk, col, x, turned, mine, sides, op, near_mine, near_sides, near_op, tiles, diag,
                      out, moved, new_diag, w_own, w_near, out_v, sem):
    samples = x.shape[0]
    slots = tiles.shape[0]
    for w, pieces in ((w_own, (mine, sides, op)), (w_near, (near_mine, near_sides, near_op))):
        at = 0
        for piece in pieces:
            w[at : at + piece.shape[0], :] = piece[...]
            at += piece.shape[0]
    scale = STEP / (2.0 * samples)
    count = meta[0]
    whole = whole_steps(count) * UNROLL
    save = lambda s: pltpu.make_async_copy(out_v.at[s], out.at[s], sem.at[s])

    def clear(s, carry):
        out_v[s] = jnp.zeros((B, B), out.dtype)
        save(s).start()
        return carry

    lax.fori_loop(whole, slots, clear, 0)

    def done_here(s):
        return jnp.logical_or(s >= count, src[s] != FAR)

    def finish(s):
        value = tiles[s].astype(F32) - gradient(s, src, blk, col, x, turned, w_own, w_near) * scale
        moved[s] = value
        out_v[s] = jnp.where(s < count, soft(value), jnp.zeros((B, B), BF16))

    def step(some):
        for s in some:
            finish(s)
        for s in some:

            @pl.when(done_here(s))
            def _():
                save(s).start()

    in_steps(count, step)
    total = column_dots(x[...], w_own[...])
    d = diag[...]
    new_diag[...] = d - STEP * (total / samples - 1.0 / d)

    def end(s, carry):
        @pl.when(done_here(s))
        def _():
            save(s).wait()

        return carry

    lax.fori_loop(0, slots, end, 0)


def own_image_kernel(first, meta, src, blk, col, x_own, x_near, tiles, acc):
    rows = pl.ds(first, acc.shape[0])
    acc[...] = jnp.zeros_like(acc)

    def add(slots):
        products = []
        for s in slots:
            at = block(blk[s])
            x = jnp.where(src[s] == NEAR, x_near[rows, at], x_own[rows, at])
            used = jnp.logical_and(s < meta[0], src[s] != FAR)
            products.append(jnp.where(used, jnp.dot(x, tiles[s], preferred_element_type=F32), 0.0))
        for s, product in zip(slots, products, strict=True):
            acc[:, block(col[s])] += product

    in_steps(meta[0], add)


def far_update_kernel(meta, src, blk, col, x, moved, *rest):
    *pieces, _, out, w, out_v, sem, found = rest
    scale = STEP / (2.0 * x.shape[0])
    at = 0
    for piece in pieces:
        w[at : at + piece.shape[0], :] = piece[...]
        at += piece.shape[0]
    count = list_of(FAR, src, meta[0], found)
    save = lambda n: pltpu.make_async_copy(out_v.at[n], out.at[found[n]], sem.at[n])

    def finish(places):
        for n in places:
            s = found[n]
            grad = over_rows(w[:, block(blk[s])], x[:, block(col[s])])
            out_v[n] = soft(moved[s] - grad * scale)
        for n in places:

            @pl.when(n < count)
            def _():
                save(n).start()

    in_steps(count, finish)
    each_live(count, lambda n: save(n).wait())


def shards(samples, theta_tiles, theta_diag, tile_row, tile_col, tile_count):
    count_ns, width = samples.shape
    blocks = width // B
    slots = theta_tiles.shape[0]
    groups = lax.axis_size("blk")
    reps = lax.axis_size("rep")
    group = lax.axis_index("blk")
    r = lax.axis_index("rep")
    quarter = count_ns // 4
    firsts = [sum(CHUNKS[:c]) for c in range(len(CHUNKS))]
    dot = 2 * count_ns * B * B

    far = [p for g in range(1, groups - 1, 2) for p in ((g, g + 1), (g + 1, g))]
    near = [p for g in range(0, groups, 2) for p in ((g, g + 1), (g + 1, g))]
    swap_far = lambda v: lax.ppermute(v, "blk", far)
    swap_near = lambda v: lax.ppermute(v, "blk", near)
    up = lambda v, n: lax.ppermute(v, "rep", [(i, (i + n) % reps) for i in range(reps)])

    rel = tile_row // blocks - group
    even = group % 2 == 0
    src = jnp.where(rel == 0, OWN, jnp.where((rel < 0) == even, FAR, NEAR)).astype(jnp.int32)
    blk = (tile_row % blocks).astype(jnp.int32)
    col = tile_col.astype(jnp.int32)
    meta = jnp.stack([tile_count[0], r.astype(jnp.int32)])
    index = (meta, src, blk, col)
    diag = theta_diag[None, :]

    x_near = swap_near(samples)
    x_first = load_first(samples, CHUNKS[0])
    x_own, *x_rest = load(samples, [(0, count_ns), *zip(firsts[1:], CHUNKS[1:], strict=True)], 10)
    x_far = [swap_far(x) for x in (x_first, *x_rest)]

    accs = [
        call(
            functools.partial(own_image_kernel, first), "own_image", like((rows, width), F32),
            [SMEM] * 4 + [VMEM] * 3, VMEM, slots * dot, 4 << 20,
        )(*index, x_own, x_near, theta_tiles)
        for first, rows in zip(firsts, CHUNKS, strict=True)
    ]
    x_rows, x_turned = call(
        reorder_kernel, "reorder", [like((count_ns, width), BF16), like((3, width, count_ns), BF16)],
        [SMEM] + [VMEM] * (2 + len(CHUNKS)), [VMEM] * 2, 0, 0,
    )(meta, x_own, x_near, *x_far)

    joined, done, before = [], 0, []
    for c, (first, rows) in enumerate(zip(firsts, CHUNKS, strict=True)):
        part = rows // 4
        own, *sends = call(
            far_image_kernel, "far_image",
            [like((part, width), F32)] + [like((part, width), BF16)] * 3,
            [SMEM] * 4 + [VMEM] * 3, [VMEM] * 4, slots * dot // 4, 1 << 20,
            [pltpu.VMEM((rows, width), F32), pltpu.SMEM((slots,), jnp.int32)],
        )(*index, accs[c], x_far[c], theta_tiles)
        got = [up(send, k + 1) for k, send in enumerate(sends)]
        if c + 1 == len(CHUNKS):
            far_first = swap_far(joined[0])
            before = [far_first, x_rows]
        joined = [
            call(
                functools.partial(combine_kernel, first, done), "combine", like((done + part, width), BF16),
                [SMEM] + [VMEM] * (6 + len(joined)) + [ANY] * len(before), VMEM, 0, 1 << 20,
            )(meta, own, *got, x_own, diag, *joined, *before)
        ]
        done += part
    w_mine = joined[0]
    w_sides, w_rest, go_up, go_down = call(
        stack_kernel, "stack",
        [like((2 * quarter, width), BF16), like((2 * quarter + part, width), BF16)]
        + [like((quarter // 2, width), BF16)] * 2,
        [VMEM] * 3, [VMEM] * 4, 0, 0,
    )(w_mine, up(w_mine, 1), up(w_mine, 3))
    far_rest = swap_far(w_rest)
    w_op = call(
        join_kernel, "join", like((quarter, width), BF16), [VMEM] * 2, VMEM, 0, 0,
    )(up(go_up, 1), up(go_down, 3))
    far_op = swap_far(w_op)
    w_own = (w_mine, w_sides, w_op)

    new_tiles, moved, new_diag = call(
        own_update_kernel, "own_update",
        [like(theta_tiles.shape, BF16), like(theta_tiles.shape, F32), like((1, width), F32)],
        [SMEM] * 4 + [VMEM] * 10, [HBM, VMEM, VMEM], 0, 0,
        [pltpu.VMEM((count_ns, width), BF16)] * 2 + [pltpu.VMEM(theta_tiles.shape, BF16), DMA((slots,))], vmem=14,
    )(*index, x_rows, x_turned, *w_own, *[swap_near(w) for w in w_own], theta_tiles, diag)

    far_pieces = [far_first, far_rest, far_op]
    new_tiles = call(
        far_update_kernel, "far_update", like(theta_tiles.shape, BF16),
        [SMEM] * 4 + [VMEM] * (2 + len(far_pieces)) + [HBM], HBM, slots * dot // 4, 2 << 20,
        [pltpu.VMEM((count_ns, width), BF16), pltpu.VMEM(theta_tiles.shape, BF16), DMA((slots,)),
         pltpu.SMEM((slots,), jnp.int32)],
        {6 + len(far_pieces): 0},
    )(*index, x_rows, moved, *far_pieces, new_tiles)
    return new_tiles, new_diag.reshape(width)


def solution(mesh):
    placed = (
        P(None, "blk"),
        P(("blk", "rep"), None, None),
        P("blk"),
        P(("blk", "rep")),
        P(("blk", "rep")),
        P(("blk", "rep")),
    )
    return jax.shard_map(
        shards,
        mesh=mesh,
        in_specs=placed,
        out_specs=(P(("blk", "rep"), None, None), P("blk")),
        check_vma=False,
    )
```

```python
import functools

import jax
import jax.numpy as jnp
from jax import lax
from jax.experimental import pallas as pl
from jax.experimental.pallas import tpu as pltpu
from jax.sharding import PartitionSpec as P

B = 256
STEP = 0.25
PENALTY = 0.5
OWN, FAR, NEAR = 0, 1, 2
HBM = pl.BlockSpec(memory_space=pltpu.HBM)
VMEM = pl.BlockSpec(memory_space=pltpu.VMEM)
SMEM = pl.BlockSpec(memory_space=pltpu.SMEM)
ANY = pl.BlockSpec(memory_space=pl.ANY)
F32, BF16 = jnp.float32, jnp.bfloat16
DMA = pltpu.SemaphoreType.DMA
OVER_ROWS = (((0,), (0,)), ((), ()))
REPS = (0, 3, 1, 2)
CHUNKS = (256, 256)


def call(kernel, name, outs, ins, out_specs, flops, moved, scratch=(), aliases=None, vmem=10):
    return pl.pallas_call(
        kernel,
        out_shape=outs,
        in_specs=ins,
        out_specs=out_specs,
        scratch_shapes=scratch,
        input_output_aliases=aliases or {},
        compiler_params=pltpu.CompilerParams(vmem_limit_bytes=int(vmem * 2**20)),
        cost_estimate=pl.CostEstimate(flops=flops, bytes_accessed=moved, transcendentals=0),
        name=name,
    )


def like(shape, dtype):
    return jax.ShapeDtypeStruct(shape, dtype)


def block(index):
    return pl.ds(pl.multiple_of(index * B, B), B)


def each_live(count, body):
    def step(s, carry):
        body(s)
        return carry

    lax.fori_loop(0, count, step, 0)


def list_of(source, src, count, found):
    def clear(n, carry):
        found[n] = 0
        return carry

    def one(s, n):
        here = src[s] == source

        @pl.when(here)
        def _():
            found[n] = s

        return n + here.astype(jnp.int32)

    lax.fori_loop(0, found.shape[0], clear, 0)
    return lax.fori_loop(0, count, one, 0)


UNROLL = 4


def whole_steps(count):
    return (count + UNROLL - 1) // UNROLL


def in_steps(count, body):
    def step(t, carry):
        body([UNROLL * t + n for n in range(UNROLL)])
        return carry

    lax.fori_loop(0, whole_steps(count), step, 0)


def over_rows(a, b):
    return lax.dot_general(a, b, OVER_ROWS, preferred_element_type=F32)


def soft(moved):
    cut = STEP * PENALTY
    return (moved - jnp.clip(moved, -cut, cut)).astype(BF16)


def load_kernel(firsts, src, *refs):
    n = len(firsts)
    copies = [
        pltpu.make_async_copy(src.at[pl.ds(first, dst.shape[0])], dst, refs[n].at[k])
        for k, (first, dst) in enumerate(zip(firsts, refs[:n], strict=True))
    ]
    for c in copies:
        c.start()
    for c in copies:
        c.wait()


def load_first_kernel(src, dst, through, in_sem, out_sem):
    pieces, rows, _ = through.shape
    ins = [pltpu.make_async_copy(src.at[pl.ds(n * rows, rows)], through.at[n], in_sem.at[n]) for n in range(pieces)]
    outs = [pltpu.make_async_copy(through.at[n], dst.at[pl.ds(n * rows, rows)], out_sem.at[n]) for n in range(pieces)]
    for c in ins:
        c.start()
    for came, goes in zip(ins, outs, strict=True):
        came.wait()
        goes.start()
    for c in outs:
        c.wait()


def load_first(src, rows):
    pieces = 4
    return call(
        load_first_kernel, "load", like((rows, src.shape[1]), src.dtype), [HBM], HBM, 0, 1 << 20,
        [pltpu.VMEM((pieces, rows // pieces, src.shape[1]), src.dtype), DMA((pieces,)), DMA((pieces,))], vmem=62.5,
    )(src)


def load(src, ranges, vmem):
    return call(
        functools.partial(load_kernel, [first for first, _ in ranges]), "load",
        [like((rows, src.shape[1]), src.dtype) for _, rows in ranges], [HBM], [VMEM] * len(ranges), 2 << 30, 1 << 20,
        [DMA((len(ranges),))], vmem=vmem,
    )(src)


def far_image_kernel(meta, src, blk, col, acc, x_far, tiles, own, send_1, send_2, send_3, total, found):
    rows = total.shape[0]
    part = rows // 4
    total[...] = acc[...]

    count = list_of(FAR, src, meta[0], found)

    def add(places):
        slots = [found[n] for n in places]
        products = [jnp.dot(x_far[:, block(blk[s])], tiles[s], preferred_element_type=F32) for s in slots]
        for n, s, product in zip(places, slots, products, strict=True):
            total[:, block(col[s])] += jnp.where(n < count, product, 0.0)

    in_steps(count, add)
    for k, out in enumerate((own, send_1, send_2, send_3)):
        at = pl.ds(pl.multiple_of(lax.rem(meta[1] + k, 4) * part, part), part)
        out[...] = total[at, :].astype(out.dtype)


def combined(first, meta, own, got, samples, diag):
    part = own.shape[0]
    at = pl.ds(pl.multiple_of(first + meta[1] * part, part), part)
    total = own[...]
    for other in got:
        total += other[:part, :].astype(F32)
    return (total + samples[at, :].astype(F32) * diag[...]).astype(BF16)


def combine_kernel(first, joined, meta, own, got_1, got_2, got_3, samples, diag, *refs):
    out = refs[-1]
    if joined:
        out[:joined, :] = refs[0][...]
    out[joined:, :] = combined(first, meta, own, (got_1, got_2, got_3), samples, diag)


def stack_kernel(mine, below, above, sides, rest, go_up, go_down):
    part = below.shape[0]
    half = part // 2
    ours = rest.shape[0] - 2 * part
    rest[:ours, :] = mine[part - ours :, :]
    for out, at in ((sides, 0), (rest, ours)):
        out[at : at + part, :] = below[...]
        out[at + part : at + 2 * part, :] = above[...]
    go_up[...] = below[:half, :]
    go_down[...] = above[half:, :]


def join_kernel(op_a, op_b, out):
    half = op_a.shape[0]
    out[:half, :] = op_a[...]
    out[half:, :] = op_b[...]


def reorder_kernel(meta, x_own, x_near, *refs):
    *x_far, out, turned = refs
    spans, first = [], 0
    for far in x_far:
        spans.append((first, far.shape[0] // 4))
        first += far.shape[0]

    def places():
        for rep in REPS:
            for c, (first, part) in enumerate(spans):
                yield c, first, pl.multiple_of(lax.rem(meta[1] + rep, 4) * part, part), part

    def turn(n, carry):
        at = block(n)
        own, far, near = [], [], []
        for c, first, row, part in places():
            own.append(x_own[pl.ds(first + row, part), at])
            far.append(x_far[c][pl.ds(row, part), at])
            near.append(x_near[pl.ds(first + row, part), at])
        own = jnp.concatenate(own, axis=0)
        out[:, at] = own
        turned[OWN, at, :] = own.T
        turned[FAR, at, :] = jnp.concatenate(far, axis=0).T
        turned[NEAR, at, :] = jnp.concatenate(near, axis=0).T
        return carry

    lax.fori_loop(0, out.shape[1] // B, turn, 0)


def gradient(s, src, blk, col, x, turned, w_own, w_near):
    k = src[s]
    at_i, at_j = block(blk[s]), block(col[s])
    one = jnp.dot(turned[k, at_i, :], w_own[:, at_j], preferred_element_type=F32)
    two = over_rows(jnp.where(k == NEAR, w_near[:, at_i], w_own[:, at_i]), x[:, at_j])
    return one + jnp.where(k == FAR, 0.0, two)


def column_dots(x, w):
    return jnp.sum(x.astype(F32) * w.astype(F32), axis=0, keepdims=True)


def own_update_kernel(meta, src, blk, col, x, turned, mine, sides, op, near_mine, near_sides, near_op, tiles, diag,
                      out, moved, new_diag, w_own, w_near, out_v, sem):
    samples = x.shape[0]
    slots = tiles.shape[0]
    for w, pieces in ((w_own, (mine, sides, op)), (w_near, (near_mine, near_sides, near_op))):
        at = 0
        for piece in pieces:
            w[at : at + piece.shape[0], :] = piece[...]
            at += piece.shape[0]
    scale = STEP / (2.0 * samples)
    count = meta[0]
    whole = whole_steps(count) * UNROLL
    save = lambda s: pltpu.make_async_copy(out_v.at[s], out.at[s], sem.at[s])

    def clear(s, carry):
        out_v[s] = jnp.zeros((B, B), out.dtype)
        save(s).start()
        return carry

    lax.fori_loop(whole, slots, clear, 0)

    def done_here(s):
        return jnp.logical_or(s >= count, src[s] != FAR)

    def finish(s):
        value = tiles[s].astype(F32) - gradient(s, src, blk, col, x, turned, w_own, w_near) * scale
        moved[s] = value
        out_v[s] = jnp.where(s < count, soft(value), jnp.zeros((B, B), BF16))

    def step(some):
        for s in some:
            finish(s)
        for s in some:

            @pl.when(done_here(s))
            def _():
                save(s).start()

    in_steps(count, step)
    total = column_dots(x[...], w_own[...])
    d = diag[...]
    new_diag[...] = d - STEP * (total / samples - 1.0 / d)

    def end(s, carry):
        @pl.when(done_here(s))
        def _():
            save(s).wait()

        return carry

    lax.fori_loop(0, slots, end, 0)


def own_image_kernel(first, meta, src, blk, col, x_own, x_near, tiles, acc):
    rows = pl.ds(first, acc.shape[0])
    acc[...] = jnp.zeros_like(acc)

    def add(slots):
        products = []
        for s in slots:
            at = block(blk[s])
            x = jnp.where(src[s] == NEAR, x_near[rows, at], x_own[rows, at])
            used = jnp.logical_and(s < meta[0], src[s] != FAR)
            products.append(jnp.where(used, jnp.dot(x, tiles[s], preferred_element_type=F32), 0.0))
        for s, product in zip(slots, products, strict=True):
            acc[:, block(col[s])] += product

    in_steps(meta[0], add)


def far_first_kernel(meta, src, blk, col, x, moved, first, rest, out, w, found):
    rows, cut = w.shape[0], first.shape[0]
    scale = STEP / (2.0 * x.shape[0])
    w[:cut, :] = first[...]
    w[cut:, :] = rest[...]
    count = list_of(FAR, src, meta[0], found)

    def add(places):
        for n in places:
            s = found[n]
            out[s] = moved[s] - over_rows(w[:, block(blk[s])], x[:rows, block(col[s])]) * scale

    in_steps(count, add)


def far_update_kernel(meta, src, blk, col, x, moved, w, _, out, out_v, sem, found):
    samples = x.shape[0]
    rows = slice(samples - w.shape[0], samples)
    scale = STEP / (2.0 * samples)
    count = list_of(FAR, src, meta[0], found)
    save = lambda n: pltpu.make_async_copy(out_v.at[n], out.at[found[n]], sem.at[n])

    def finish(places):
        for n in places:
            s = found[n]
            grad = over_rows(w[:, block(blk[s])], x[rows, block(col[s])])
            out_v[n] = soft(moved[s] - grad * scale)
        for n in places:

            @pl.when(n < count)
            def _():
                save(n).start()

    in_steps(count, finish)
    each_live(count, lambda n: save(n).wait())


def shards(samples, theta_tiles, theta_diag, tile_row, tile_col, tile_count):
    count_ns, width = samples.shape
    blocks = width // B
    slots = theta_tiles.shape[0]
    groups = lax.axis_size("blk")
    reps = lax.axis_size("rep")
    group = lax.axis_index("blk")
    r = lax.axis_index("rep")
    quarter = count_ns // 4
    firsts = [sum(CHUNKS[:c]) for c in range(len(CHUNKS))]
    dot = 2 * count_ns * B * B

    far = [p for g in range(1, groups - 1, 2) for p in ((g, g + 1), (g + 1, g))]
    near = [p for g in range(0, groups, 2) for p in ((g, g + 1), (g + 1, g))]
    swap_far = lambda v: lax.ppermute(v, "blk", far)
    swap_near = lambda v: lax.ppermute(v, "blk", near)
    up = lambda v, n: lax.ppermute(v, "rep", [(i, (i + n) % reps) for i in range(reps)])

    rel = tile_row // blocks - group
    even = group % 2 == 0
    src = jnp.where(rel == 0, OWN, jnp.where((rel < 0) == even, FAR, NEAR)).astype(jnp.int32)
    blk = (tile_row % blocks).astype(jnp.int32)
    col = tile_col.astype(jnp.int32)
    meta = jnp.stack([tile_count[0], r.astype(jnp.int32)])
    index = (meta, src, blk, col)
    diag = theta_diag[None, :]

    x_near = swap_near(samples)
    x_first = load_first(samples, CHUNKS[0])
    x_own, *x_rest = load(samples, [(0, count_ns), *zip(firsts[1:], CHUNKS[1:], strict=True)], 10)
    x_far = [swap_far(x) for x in (x_first, *x_rest)]

    accs = [
        call(
            functools.partial(own_image_kernel, first), "own_image", like((rows, width), F32),
            [SMEM] * 4 + [VMEM] * 3, VMEM, slots * dot, 4 << 20,
        )(*index, x_own, x_near, theta_tiles)
        for first, rows in zip(firsts, CHUNKS, strict=True)
    ]
    x_rows, x_turned = call(
        reorder_kernel, "reorder", [like((count_ns, width), BF16), like((3, width, count_ns), BF16)],
        [SMEM] + [VMEM] * (2 + len(CHUNKS)), [VMEM] * 2, 0, 0,
    )(meta, x_own, x_near, *x_far)

    joined, done, before = [], 0, []
    for c, (first, rows) in enumerate(zip(firsts, CHUNKS, strict=True)):
        part = rows // 4
        own, *sends = call(
            far_image_kernel, "far_image",
            [like((part, width), F32)] + [like((part, width), BF16)] * 3,
            [SMEM] * 4 + [VMEM] * 3, [VMEM] * 4, slots * dot // 4, 1 << 20,
            [pltpu.VMEM((rows, width), F32), pltpu.SMEM((slots,), jnp.int32)],
        )(*index, accs[c], x_far[c], theta_tiles)
        got = [up(send, k + 1) for k, send in enumerate(sends)]
        if c + 1 == len(CHUNKS):
            far_first = swap_far(joined[0])
            before = [far_first, x_rows]
        joined = [
            call(
                functools.partial(combine_kernel, first, done), "combine", like((done + part, width), BF16),
                [SMEM] + [VMEM] * (6 + len(joined)) + [ANY] * len(before), VMEM, 0, 1 << 20,
            )(meta, own, *got, x_own, diag, *joined, *before)
        ]
        done += part
    w_mine = joined[0]
    w_sides, w_rest, go_up, go_down = call(
        stack_kernel, "stack",
        [like((2 * quarter, width), BF16), like((2 * quarter + part, width), BF16)]
        + [like((quarter // 2, width), BF16)] * 2,
        [VMEM] * 3, [VMEM] * 4, 0, 0,
    )(w_mine, up(w_mine, 1), up(w_mine, 3))
    far_rest = swap_far(w_rest)
    w_op = call(
        join_kernel, "join", like((quarter, width), BF16), [VMEM] * 2, VMEM, 0, 0,
    )(up(go_up, 1), up(go_down, 3))
    far_op = swap_far(w_op)
    w_own = (w_mine, w_sides, w_op)

    new_tiles, moved, new_diag = call(
        own_update_kernel, "own_update",
        [like(theta_tiles.shape, BF16), like(theta_tiles.shape, F32), like((1, width), F32)],
        [SMEM] * 4 + [VMEM] * 10, [HBM, VMEM, VMEM], 0, 0,
        [pltpu.VMEM((count_ns, width), BF16)] * 2 + [pltpu.VMEM(theta_tiles.shape, BF16), DMA((slots,))], vmem=14,
    )(*index, x_rows, x_turned, *w_own, *[swap_near(w) for w in w_own], theta_tiles, diag)

    moved = call(
        far_first_kernel, "far_first", like(theta_tiles.shape, F32), [SMEM] * 4 + [VMEM] * 4, VMEM, 0, 0,
        [pltpu.VMEM((3 * quarter, width), BF16), pltpu.SMEM((slots,), jnp.int32)],
    )(*index, x_rows, moved, far_first, far_rest)
    new_tiles = call(
        far_update_kernel, "far_update", like(theta_tiles.shape, BF16),
        [SMEM] * 4 + [VMEM] * 3 + [HBM], HBM, 0, 0,
        [pltpu.VMEM(theta_tiles.shape, BF16), DMA((slots,)), pltpu.SMEM((slots,), jnp.int32)], {7: 0},
    )(*index, x_rows, moved, far_op, new_tiles)
    return new_tiles, new_diag.reshape(width)


def solution(mesh):
    placed = (
        P(None, "blk"),
        P(("blk", "rep"), None, None),
        P("blk"),
        P(("blk", "rep")),
        P(("blk", "rep")),
        P(("blk", "rep")),
    )
    return jax.shard_map(
        shards,
        mesh=mesh,
        in_specs=placed,
        out_specs=(P(("blk", "rep"), None, None), P("blk")),
        check_vma=False,
    )
```
